32 devices in a mesh: section: 4 (over y, x), seq: 4 (over z), tensor: 2 (over core).
Axes of the slice: x: 2, y: 2, z: 4, core: 2. Of those that a mesh axis runs over, the one named last changes fastest.
Arguments:
- values: bfloat16 [1024, 8192], P('seq', ('section', 'tensor')), may hold values from -6 to 6
- gate_in: bfloat16 [1024, 8192], P('seq', ('section', 'tensor')), may hold values from -6 to 6
- b_proj: bfloat16 [1024, 4, 128], P('seq', 'section'), may hold values from -0.5 to 0.5
- c_proj: bfloat16 [1024, 4, 128], P('seq', 'section'), may hold values from -0.5 to 0.5
- step_size: float32 [128, 1024], P(('section', 'tensor'), 'seq'), may hold values from 0.25 to 2
- decay_rate: float32 [128], P(('section', 'tensor')), may hold values from 0.0009765625 to 0.1
- norm_gain: float32 [8192], P(('section', 'tensor')), may hold values from 0.5 to 1.5
- cotangent: bfloat16 [1024, 8192], P('seq', ('section', 'tensor')), may hold values from -6 to 6
Outputs:
- result: bfloat16 [1024, 8192], P('seq', ('section', 'tensor'))
- grad_values: bfloat16 [1024, 8192], P('seq', ('section', 'tensor'))
- grad_gate: bfloat16 [1024, 8192], P('seq', ('section', 'tensor'))
- grad_b: float32 [1024, 4, 128], P('seq', 'section')
- grad_c: float32 [1024, 4, 128], P('seq', 'section')
- grad_step: float32 [128, 1024], P(('section', 'tensor'), 'seq')
- grad_rate: float32 [128], P(('section', 'tensor'))
- grad_gain: float32 [8192], P(('section', 'tensor'))
The draws below stay inside these ranges and needn't reach their ends.
All inputs are finite; a program needn't handle non-finite values.
Results may differ from the reference program's by a relative error of at most 0.001.
Values sent between devices are 32-bit elements; how exact they have to be, the bound alone decides.
A program may use at most 128 MiB of HBM per device.

```python
import math
import jax
import jax.numpy as jnp
from jax import lax

HEADS = 128
P_SIZE = 64
N = 128
GROUPS = 4
BLOCK = 128
TOKENS = 1024


def shard_levels(stream_key, dims, split, smallest, top_value):
    loudness = 1.0
    for axis_at, blocks in split:
        steps = jax.random.uniform(jax.random.fold_in(jax.random.fold_in(stream_key, 6), axis_at), (blocks,), jnp.float32, smallest / len(split), top_value / len(split))
        loudness = loudness * jnp.repeat(jnp.exp(steps), dims[axis_at] // blocks).reshape((-1,) + (1,) * (len(dims) - 1 - axis_at))
    return loudness


def normal_values(rng, dims, deviation, most, pieces=(), held_as=jnp.bfloat16):
    entries = jax.random.normal(rng, dims, jnp.float32) * deviation
    if len(pieces) > 0:
        entries = shard_levels(rng, dims, pieces, -0.22, 0.18) * entries
    return jnp.clip(entries, min=-most, max=most).astype(held_as)


def setup_inputs(seed: int = 0) -> dict:
    seeds = jax.random.split(jax.random.key(seed), 9)
    values = normal_values(seeds[0], (TOKENS, HEADS * P_SIZE), 1.0, 6.0, ((0, 4), (1, 8)))
    gate_in = normal_values(seeds[1], (TOKENS, HEADS * P_SIZE), 1.0, 6.0, ((0, 4), (1, 8)))
    b_proj = normal_values(seeds[2], (TOKENS, GROUPS, N), N ** -0.5, 0.5, ((0, 4), (1, 4)))
    c_proj = normal_values(seeds[3], (TOKENS, GROUPS, N), N ** -0.5, 0.5, ((0, 4), (1, 4)))
    step_size = jnp.clip(jnp.exp(math.log(2.0) - 2.0794415 * jax.random.uniform(seeds[4], (HEADS, TOKENS), jnp.float32) ** shard_levels(seeds[4], (HEADS, TOKENS), ((0, 8), (1, 4)), -0.2, 0.2)), 0.25, 2.0)
    decay_rate = jnp.clip(jnp.exp(math.log(0.1) - 4.6288867 * jax.random.uniform(seeds[5], (HEADS,), jnp.float32) ** shard_levels(seeds[5], (HEADS,), ((0, 8),), -0.2, 0.2)), 0.0009765625, 0.1)
    norm_gain = jnp.clip(1.0 + 0.1 * jax.random.normal(seeds[6], (HEADS * P_SIZE,), jnp.float32), 0.5, 1.5)
    cotangent = normal_values(seeds[7], (TOKENS, HEADS * P_SIZE), 1.0, 6.0, ((0, 4), (1, 8)))
    return {"values": values, "gate_in": gate_in, "b_proj": b_proj, "c_proj": c_proj, "step_size": step_size, "decay_rate": decay_rate, "norm_gain": norm_gain, "cotangent": cotangent}


HIGHEST = lax.Precision.HIGHEST
EPSILON = 1e-05
CLIP = 90.0

def block_scan(inputs_h, b_rows, c_rows, steps_dt, rates, state_in):
    length = inputs_h.shape[0]
    heads = inputs_h.shape[1]
    blocks = length // BLOCK
    value_blocks = inputs_h.reshape(blocks, BLOCK, heads, P_SIZE)
    b_blocks = b_rows.reshape(blocks, BLOCK, N)
    c_blocks = c_rows.reshape(blocks, BLOCK, N)
    dt_blocks = steps_dt.reshape(heads, blocks, BLOCK).transpose(1, 0, 2)
    position = jnp.arange(BLOCK)
    causal = (position[:, None] >= position[None, :])[None]

    def advance(state, item):
        value_blk, b_blk, c_blk, dt_blk = item
        cumulative = jnp.cumsum(-dt_blk * rates[:, None], axis=1)
        spread = cumulative[:, :, None] - cumulative[:, None, :]
        segment = jnp.where(causal, jnp.exp(jnp.where(causal, spread, 0.0)), 0.0)
        intersection_m = jnp.dot(c_blk, b_blk.T, precision=HIGHEST, preferred_element_type=jnp.float32)
        weights = intersection_m[None] * segment * dt_blk[:, None, :]
        inner = jnp.einsum('hij,jhp->ihp', weights, value_blk, precision=HIGHEST)
        carried = jnp.einsum('in,hnp->ihp', c_blk, state, precision=HIGHEST) * jnp.exp(cumulative).T[:, :, None]
        tail = jnp.exp(cumulative[:, -1:] - cumulative) * dt_blk
        fresh = jnp.exp(cumulative[:, -1])[:, None, None] * state + jnp.einsum('hj,jn,jhp->hnp', tail, b_blk, value_blk, precision=HIGHEST)
        return (fresh, inner + carried)
    state_out, outputs = lax.scan(jax.checkpoint(advance), state_in, (value_blocks, b_blocks, c_blocks, dt_blocks))
    return (outputs.reshape(length, heads, P_SIZE), state_out)

def forward(values, gate_in, b_proj, c_proj, step_size, decay_rate, norm_gain):
    heads_group = HEADS // GROUPS
    grouped = values.reshape(TOKENS, GROUPS, heads_group, P_SIZE).transpose(1, 0, 2, 3)
    b_group = b_proj.transpose(1, 0, 2)
    c_group = c_proj.transpose(1, 0, 2)
    dt_group = step_size.reshape(GROUPS, heads_group, TOKENS)
    rate_group = decay_rate.reshape(GROUPS, heads_group)

    def one_group(item):
        group_vals, group_b, group_c, group_dt, group_rate = item
        start = jnp.zeros((heads_group, N, P_SIZE), jnp.float32)
        return block_scan(group_vals, group_b, group_c, group_dt, group_rate, start)[0]
    mixed = lax.map(one_group, (grouped, b_group, c_group, dt_group, rate_group))
    mixed = mixed.transpose(1, 0, 2, 3).reshape(TOKENS, HEADS * P_SIZE)
    gated = mixed * jax.nn.silu(gate_in)
    shaped = gated.reshape(TOKENS, GROUPS, HEADS * P_SIZE // GROUPS)
    scale = lax.rsqrt(lax.optimization_barrier(jnp.mean(shaped * shaped, axis=2)) + EPSILON)
    return (shaped * scale[:, :, None]).reshape(TOKENS, HEADS * P_SIZE) * norm_gain

def reference(values, gate_in, b_proj, c_proj, step_size, decay_rate, norm_gain, cotangent):
    result, pullback = jax.vjp(forward, values.astype(jnp.float32), gate_in.astype(jnp.float32), b_proj.astype(jnp.float32), c_proj.astype(jnp.float32), step_size, decay_rate, norm_gain)
    grads = pullback(cotangent.astype(jnp.float32))
    total = jnp.sum(grads[5] * grads[5]) + jnp.sum(grads[6] * grads[6])
    factor = CLIP / jnp.maximum(jnp.sqrt(total), CLIP)
    return (result.astype(jnp.bfloat16), grads[0].astype(jnp.bfloat16), grads[1].astype(jnp.bfloat16), grads[2], grads[3], grads[4], grads[5] * factor, grads[6] * factor)
```

```python
import functools
import jax
import jax.numpy as jnp
from jax import lax
from jax.experimental import pallas as pl
from jax.experimental.pallas import tpu as pltpu
from jax.sharding import PartitionSpec as P

P_SIZE = 64
N = 128
EPSILON = 1e-05
CLIP = 90.0
WIDE = 256
HOP = 128
F32 = jnp.float32
BF16 = jnp.bfloat16
MESH = pl.DeviceIdType.MESH


def nn(a, b):
    return lax.dot_general(a, b, (((1,), (0,)), ((), ())), preferred_element_type=F32)


def nt(a, b):
    return lax.dot_general(a, b, (((1,), (1,)), ((), ())), preferred_element_type=F32)


def split2(x):
    hi = x.astype(BF16)
    return hi, (x - hi.astype(F32)).astype(BF16)


def split3(x):
    hi = x.astype(BF16).astype(F32)
    rest = x - hi
    mid = rest.astype(BF16).astype(F32)
    return hi, mid, rest - mid


def stacked3(x):
    return jnp.concatenate(split3(x), axis=0)


def unstack3(x):
    h = x.shape[0] // 3
    return x[0:h] + x[h : 2 * h] + x[2 * h :]


def kernel(
    sizes,
    v_ref, g_ref, b_ref, c_ref, dt_ref, r_ref, gain_ref, cot_ref,
    res_ref, gv_ref, gg_ref, gb_ref, gc_ref, gs_ref, gr_ref, ggain_ref,
    pex, qex, xhi, xlo, ehi, elo, mix, zd, mte, swi, dsw,
    bx, sin, sout, ce, gin, gout, sq, inn, dm, dca, dba,
    bt, ct, m_hi, m_lo, mt_hi, mt_lo,
    stb, dcb, dbb, gainb, rateb, scb,
    fs, fr, bs, br, st_s, st_r, dc_s, dc_r, db_s, db_r, ga_s, ga_r, ra_s, ra_r, sc_s, sc_r,
):
    n_sec, n_seq, n_ten = sizes
    tokens, channels = v_ref.shape
    heads = dt_ref.shape[0]
    width = WIDE if channels % WIDE == 0 else HOP
    chunks = channels // width
    hops = channels // HOP
    seq = lax.axis_index("seq")
    ten = lax.axis_index("tensor")
    lin = lax.axis_index("section") * n_ten + ten
    n_lin = n_sec * n_ten

    def seq_peer(i):
        return {"seq": i}

    def ten_peer(i):
        return {"tensor": i}

    def lin_peer(i):
        return {"section": i // n_ten, "tensor": i % n_ten}

    barrier = pltpu.get_barrier_semaphore()
    for d in range(1, n_seq):
        pl.semaphore_signal(barrier, inc=1, device_id=seq_peer((seq + d) % n_seq), device_id_type=MESH)
    for d in range(1, n_lin):
        pl.semaphore_signal(barrier, inc=1, device_id=lin_peer((lin + d) % n_lin), device_id_type=MESH)

    def send_all(buf, me, count, peer, ssem, rsem):
        for d in range(1, count):
            pltpu.make_async_remote_copy(
                src_ref=buf.at[me], dst_ref=buf.at[me], send_sem=ssem.at[d - 1], recv_sem=rsem.at[d - 1],
                device_id=peer((me + d) % count), device_id_type=MESH,
            ).start()

    def wait_all(buf, me, count, peer, ssem, rsem):
        for d in range(1, count):
            other = (me + count - d) % count
            desc = pltpu.make_async_remote_copy(
                src_ref=buf.at[me], dst_ref=buf.at[other], send_sem=ssem.at[d - 1], recv_sem=rsem.at[d - 1],
                device_id=peer((me + d) % count), device_id_type=MESH,
            )
            desc.wait_send()
            desc.wait_recv()

    def total_of(buf, count):
        out = buf[0]
        for i in range(1, count):
            out = out + buf[i]
        return out

    def at(c):
        return pl.ds(pl.multiple_of(c * width, width), width)

    def loop(body):
        def step(c, carry):
            body(c, at(c))
            return carry

        lax.fori_loop(0, chunks, step, 0)

    def picks(rows, c):
        row = lax.broadcasted_iota(jnp.int32, (rows, width), 0) & (heads - 1)
        col = lax.broadcasted_iota(jnp.int32, (rows, width), 1) // P_SIZE + c * (width // P_SIZE)
        return jnp.where(row == col, 1.0, 0.0)

    eye = lax.broadcasted_iota(jnp.int32, (heads, heads), 0) == lax.broadcasted_iota(jnp.int32, (heads, heads), 1)
    rate = jnp.sum(jnp.where(eye, r_ref[...], 0.0), axis=1, keepdims=True)
    dt = dt_ref[...]
    row_t = lax.broadcasted_iota(jnp.int32, (tokens, tokens), 0)
    col_t = lax.broadcasted_iota(jnp.int32, (tokens, tokens), 1)
    lower = row_t >= col_t
    upper = row_t <= col_t
    cum = unstack3(nn(stacked3(-dt * rate).astype(BF16), jnp.where(upper, 1.0, 0.0).astype(BF16)))
    p3 = stacked3(jnp.exp(cum)).T.astype(BF16)
    q3 = stacked3(jnp.exp(-cum) * dt).T.astype(BF16)
    bt[...] = b_ref[...].astype(F32).T.astype(BF16)
    ct[...] = c_ref[...].astype(F32).T.astype(BF16)

    def first(c, cols):
        sel = picks(3 * heads, c).astype(BF16)
        pex[:, cols] = nn(p3, sel)
        qx = nn(q3, sel)
        qex[:, cols] = qx
        hi, lo = split2(qx * v_ref[:, cols].astype(F32))
        xhi[:, cols] = hi
        xlo[:, cols] = lo
        bx[:, cols] = nn(bt[...], hi) + nn(bt[...], lo)

    loop(first)

    @pl.when(seq == 0)
    def _():
        sin[...] = jnp.zeros_like(sin)

    @pl.when(seq == n_seq - 1)
    def _():
        gin[...] = jnp.zeros_like(gin)

    pl.semaphore_wait(barrier, n_seq - 1 + n_lin - 1)

    def forward_hop(k):
        cols = pl.ds(k * HOP, HOP)
        return pltpu.make_async_remote_copy(
            src_ref=sout.at[:, cols], dst_ref=sin.at[:, cols], send_sem=fs.at[k], recv_sem=fr.at[k],
            device_id=seq_peer((seq + 1) % n_seq), device_id_type=MESH,
        )

    def backward_hop(k):
        cols = pl.ds(k * HOP, HOP)
        return pltpu.make_async_remote_copy(
            src_ref=gout.at[:, cols], dst_ref=gin.at[:, cols], send_sem=bs.at[k], recv_sem=br.at[k],
            device_id=seq_peer((seq + n_seq - 1) % n_seq), device_id_type=MESH,
        )

    def total_decay(cols):
        return pex[tokens - 1 : tokens, cols]

    @pl.when(seq == 0)
    def _():
        for k in range(hops):
            cols = pl.ds(k * HOP, HOP)
            sout[:, cols] = total_decay(cols) * bx[:, cols]
            forward_hop(k).start()

    cb = nt(c_ref[...], b_ref[...])
    hi, lo = split2(jnp.where(lower, cb, 0.0))
    m_hi[...] = hi
    m_lo[...] = lo
    bc = nt(b_ref[...], c_ref[...])
    hi, lo = split2(jnp.where(upper, bc, 0.0))
    mt_hi[...] = hi
    mt_lo[...] = lo

    def second(c, cols):
        gate = g_ref[:, cols].astype(F32)
        sigm = 1.0 / (1.0 + jnp.exp(-gate))
        swi[:, cols] = gate * sigm
        dsw[:, cols] = sigm * (1.0 + gate * (1.0 - sigm))
        x_hi = xhi[:, cols]
        mix[:, cols] = nn(m_hi[...], x_hi) + (nn(m_hi[...], xlo[:, cols]) + nn(m_lo[...], x_hi))

    loop(second)

    @pl.when(seq > 0)
    def _():
        for k in range(hops):
            cols = pl.ds(k * HOP, HOP)
            forward_hop(k).wait_recv()

            @pl.when(seq < n_seq - 1)
            def _():
                sout[:, cols] = total_decay(cols) * (sin[:, cols] + bx[:, cols])
                forward_hop(k).start()

    sq[...] = jnp.zeros_like(sq)
    inn[...] = jnp.zeros_like(inn)

    def third(c, cols):
        hi, lo = split2(sin[:, cols])
        mixed = pex[:, cols] * (mix[:, cols] + (nn(c_ref[...], hi) + nn(c_ref[...], lo)))
        mix[:, cols] = mixed
        gated = mixed * swi[:, cols]
        squares = gated * gated
        products = cot_ref[:, cols].astype(F32) * gain_ref[:, cols] * gated
        for part in range(width // HOP):
            piece = slice(part * HOP, (part + 1) * HOP)
            sq[...] += squares[:, piece]
            inn[...] += products[:, piece]

    loop(third)

    lane = lax.broadcasted_iota(jnp.int32, (tokens, 128), 1)
    stb[ten] = jnp.where(
        lane < 64, jnp.sum(sq[...], axis=1, keepdims=True), jnp.sum(inn[...], axis=1, keepdims=True)
    )
    send_all(stb, ten, n_ten, ten_peer, st_s, st_r)
    wait_all(stb, ten, n_ten, ten_peer, st_s, st_r)
    sums = total_of(stb, n_ten)
    group_width = channels * n_ten
    scale = lax.rsqrt(sums[:, 0:1] / group_width + EPSILON)
    pull = scale * scale * scale * sums[:, 64:65] / group_width

    def fourth(c, cols):
        mixed = mix[:, cols]
        swish = swi[:, cols]
        gated = mixed * swish
        d_gated = scale * (cot_ref[:, cols].astype(F32) * gain_ref[:, cols]) - gated * pull
        gg_ref[:, cols] = (d_gated * mixed * dsw[:, cols]).astype(BF16)
        d_mixed = d_gated * swish
        zd[:, cols] = d_mixed * mixed
        hi, lo = split2(pex[:, cols] * d_mixed)
        ehi[:, cols] = hi
        elo[:, cols] = lo
        ce[:, cols] = nn(ct[...], hi) + nn(ct[...], lo)

    loop(fourth)

    @pl.when(seq == n_seq - 1)
    def _():
        for k in range(hops):
            cols = pl.ds(k * HOP, HOP)
            gout[:, cols] = ce[:, cols]
            backward_hop(k).start()

    dm[...] = jnp.zeros_like(dm)
    dca[...] = jnp.zeros_like(dca)

    def fifth(c, cols):
        e_hi = ehi[:, cols]
        e_lo = elo[:, cols]
        x_hi = xhi[:, cols]
        mte[:, cols] = nn(mt_hi[...], e_hi) + (nn(mt_hi[...], e_lo) + nn(mt_lo[...], e_hi))
        dm[...] += nt(e_hi, x_hi) + (nt(e_hi, xlo[:, cols]) + nt(e_lo, x_hi))
        s_hi, s_lo = split2(sin[:, cols])
        dca[...] += nt(e_hi, s_hi) + (nt(e_hi, s_lo) + nt(e_lo, s_hi))
        normed = mix[:, cols] * swi[:, cols] * scale
        res_ref[:, cols] = (normed * gain_ref[:, cols]).astype(BF16)
        gain_sum = jnp.sum(cot_ref[:, cols].astype(F32) * normed, axis=0, keepdims=True)
        gainb[seq, :, cols] = jnp.broadcast_to(gain_sum, (8, width))

    loop(fifth)
    send_all(gainb, seq, n_seq, seq_peer, ga_s, ga_r)
    d_m = jnp.where(lower, dm[...], 0.0)
    hi, lo = split2(d_m)
    dcb[ten] = dca[...] + (nn(hi, b_ref[...]) + nn(lo, b_ref[...]))
    send_all(dcb, ten, n_ten, ten_peer, dc_s, dc_r)
    hi, lo = split2(d_m.T)
    dba[...] = nn(hi, c_ref[...]) + nn(lo, c_ref[...])

    @pl.when(seq < n_seq - 1)
    def _():
        for k in range(hops):
            cols = pl.ds(k * HOP, HOP)
            backward_hop(k).wait_recv()

            @pl.when(seq > 0)
            def _():
                gout[:, cols] = ce[:, cols] + total_decay(cols) * gin[:, cols]
                backward_hop(k).start()

    def sixth(c, carry):
        cols = at(c)
        row_sum, direct, end = carry
        e_grad = total_decay(cols) * gin[:, cols]
        hi, lo = split2(e_grad)
        d_v = qex[:, cols] * (mte[:, cols] + (nn(b_ref[...], hi) + nn(b_ref[...], lo)))
        gv_ref[:, cols] = d_v.astype(BF16)
        x_hi = xhi[:, cols]
        dba[...] += nt(x_hi, hi) + (nt(x_hi, lo) + nt(xlo[:, cols], hi))
        own = d_v * v_ref[:, cols].astype(F32)
        sel = picks(heads, c)
        pick = sel.astype(BF16)
        a, b, d = split3(zd[:, cols] - own)
        row_sum = row_sum + (nt(pick, a.astype(BF16)) + nt(pick, b.astype(BF16)) + nt(pick, d.astype(BF16)))
        hi, lo = split2(own)
        direct = direct + (nt(pick, hi) + nt(pick, lo))
        column = jnp.sum(e_grad * (sin[:, cols] + bx[:, cols]), axis=0, keepdims=True)
        end = end + jnp.sum(sel * column, axis=1, keepdims=True)
        return row_sum, direct, end

    zero = jnp.zeros((heads, tokens), F32)
    row_sum, direct, end = lax.fori_loop(0, chunks, sixth, (zero, zero, jnp.zeros((heads, 1), F32)))
    dbb[ten] = dba[...]
    send_all(dbb, ten, n_ten, ten_peer, db_s, db_r)
    tail = unstack3(nn(stacked3(row_sum).astype(BF16), jnp.where(lower, 1.0, 0.0).astype(BF16))) + end
    rateb[seq] = jnp.broadcast_to(-jnp.sum(dt * tail, axis=1, keepdims=True), (heads, 128))
    send_all(rateb, seq, n_seq, seq_peer, ra_s, ra_r)
    gs_ref[...] = direct / dt - rate * tail
    wait_all(gainb, seq, n_seq, seq_peer, ga_s, ga_r)
    gain_total = total_of(gainb, n_seq)[0:1]
    gain_square = jnp.sum(gain_total * gain_total, axis=1, keepdims=True)
    wait_all(rateb, seq, n_seq, seq_peer, ra_s, ra_r)
    rate_total = total_of(rateb, n_seq)
    scb[lin] = jnp.broadcast_to(jnp.sum(rate_total * rate_total, axis=0, keepdims=True) + gain_square, (8, 128))
    send_all(scb, lin, n_lin, lin_peer, sc_s, sc_r)
    wait_all(dcb, ten, n_ten, ten_peer, dc_s, dc_r)
    gc_ref[...] = total_of(dcb, n_ten)
    wait_all(dbb, ten, n_ten, ten_peer, db_s, db_r)
    gb_ref[...] = total_of(dbb, n_ten)

    @pl.when(seq < n_seq - 1)
    def _():
        for k in range(hops):
            forward_hop(k).wait_send()

    @pl.when(seq > 0)
    def _():
        for k in range(hops):
            backward_hop(k).wait_send()

    wait_all(scb, lin, n_lin, lin_peer, sc_s, sc_r)
    total = total_of(scb, n_lin)
    factor = CLIP / jnp.maximum(jnp.sqrt(total), CLIP)
    ggain_ref[...] = gain_total * factor[0:1, 0:1]
    line = lax.broadcasted_iota(jnp.int32, (heads, 128), 0) == lax.broadcasted_iota(jnp.int32, (heads, 128), 1)
    gr_ref[...] = jnp.sum(jnp.where(line, rate_total * factor[0:1], 0.0), axis=0, keepdims=True)


def local(values, gate_in, b_proj, c_proj, step_size, decay_rate, norm_gain, cotangent):
    n_sec, n_seq, n_ten = lax.axis_size("section"), lax.axis_size("seq"), lax.axis_size("tensor")
    n_lin = n_sec * n_ten
    tokens, channels = values.shape
    heads = decay_rate.shape[0]
    hops = channels // HOP
    shape = jax.ShapeDtypeStruct
    vm = pltpu.VMEM
    wide32 = vm((tokens, channels), F32)
    wide16 = vm((tokens, channels), BF16)
    state = vm((N, channels), F32)
    square16 = vm((tokens, tokens), BF16)
    slim = vm((tokens, 128), F32)
    sems = pltpu.SemaphoreType.DMA
    outs = pl.pallas_call(
        functools.partial(kernel, (n_sec, n_seq, n_ten)),
        out_shape=(
            shape((tokens, channels), BF16),
            shape((tokens, channels), BF16),
            shape((tokens, channels), BF16),
            shape((tokens, N), F32),
            shape((tokens, N), F32),
            shape((heads, tokens), F32),
            shape((1, 128), F32),
            shape((1, channels), F32),
        ),
        in_specs=[pl.BlockSpec(memory_space=vm)] * 8,
        out_specs=[pl.BlockSpec(memory_space=vm)] * 8,
        scratch_shapes=[
            wide32, wide32, wide16, wide16, wide16, wide16, wide32, wide32, wide32, wide32, wide32,
            state, state, state, state, state, state, slim, slim, vm((tokens, tokens), F32), slim, slim,
            vm((N, tokens), BF16), vm((N, tokens), BF16), square16, square16, square16, square16,
            vm((n_ten, tokens, 128), F32), vm((n_ten, tokens, 128), F32), vm((n_ten, tokens, 128), F32),
            vm((n_seq, 8, channels), F32), vm((n_seq, heads, 128), F32), vm((n_lin, 8, 128), F32),
            sems((hops,)), sems((hops,)), sems((hops,)), sems((hops,)),
            sems((n_ten,)), sems((n_ten,)), sems((n_ten,)), sems((n_ten,)), sems((n_ten,)), sems((n_ten,)),
            sems((n_seq,)), sems((n_seq,)), sems((n_seq,)), sems((n_seq,)), sems((n_lin,)), sems((n_lin,)),
        ],
        compiler_params=pltpu.CompilerParams(
            collective_id=0, has_side_effects=True, vmem_limit_bytes=48 * 1024 * 1024
        ),
    )(
        values, gate_in, b_proj[:, 0, :], c_proj[:, 0, :], step_size,
        decay_rate[None, :], norm_gain[None, :], cotangent,
    )
    result, grad_values, grad_gate, grad_b, grad_c, grad_step, grad_rate, grad_gain = outs
    return (
        result, grad_values, grad_gate, grad_b[:, None, :], grad_c[:, None, :], grad_step,
        grad_rate[0, :heads], grad_gain[0],
    )


def solution(mesh):
    return jax.shard_map(
        local,
        mesh=mesh,
        in_specs=(
            P("seq", ("section", "tensor")),
            P("seq", ("section", "tensor")),
            P("seq", "section", None),
            P("seq", "section", None),
            P(("section", "tensor"), "seq"),
            P(("section", "tensor")),
            P(("section", "tensor")),
            P("seq", ("section", "tensor")),
        ),
        out_specs=(
            P("seq", ("section", "tensor")),
            P("seq", ("section", "tensor")),
            P("seq", ("section", "tensor")),
            P("seq", "section", None),
            P("seq", "section", None),
            P(("section", "tensor"), "seq"),
            P(("section", "tensor")),
            P(("section", "tensor")),
        ),
        check_vma=False,
    )
```

```python
import functools
import jax
import jax.numpy as jnp
from jax import lax
from jax.experimental import pallas as pl
from jax.experimental.pallas import tpu as pltpu
from jax.sharding import PartitionSpec as P

P_SIZE = 64
N = 128
EPSILON = 1e-05
CLIP = 90.0
WIDE = 256
HOP = 128
F32 = jnp.float32
BF16 = jnp.bfloat16
MESH = pl.DeviceIdType.MESH


def nn(a, b):
    return lax.dot_general(a, b, (((1,), (0,)), ((), ())), preferred_element_type=F32)


def nt(a, b):
    return lax.dot_general(a, b, (((1,), (1,)), ((), ())), preferred_element_type=F32)


def split2(x):
    hi = x.astype(BF16)
    return hi, (x - hi.astype(F32)).astype(BF16)


def split3(x):
    hi = x.astype(BF16).astype(F32)
    rest = x - hi
    mid = rest.astype(BF16).astype(F32)
    return hi, mid, rest - mid


def stacked3(x):
    return jnp.concatenate(split3(x), axis=0)


def unstack3(x):
    h = x.shape[0] // 3
    return x[0:h] + x[h : 2 * h] + x[2 * h :]


def kernel(
    sizes,
    v_in, g_in, b_in, c_in, dt_in, r_in, gain_in, cot_in,
    res_ref, gv_ref, gg_ref, gb_ref, gc_ref, gs_ref, gr_ref, ggain_ref,
    pex, qex, xhi, xlo, ehi, elo, mix, zd, mte, swi, dsw,
    bx, sin, sout, ce, gin, gout, sq, inn, dm, dca, dba,
    bt, ct, m_hi, m_lo, mt_hi, mt_lo,
    stb, dcb, dbb, gainb, rateb, scb,
    v_ref, g_ref, b_ref, c_ref, dt_ref, r_ref, gain_ref, cot_ref, loads,
    fs, fr, bs, br, st_s, st_r, dc_s, dc_r, db_s, db_r, ga_s, ga_r, ra_s, ra_r, sc_s, sc_r,
):
    n_sec, n_seq, n_ten = sizes
    tokens, channels = v_ref.shape
    heads = dt_ref.shape[0]
    width = WIDE if channels % WIDE == 0 else HOP
    chunks = channels // width
    hops = channels // HOP
    seq = lax.axis_index("seq")
    ten = lax.axis_index("tensor")
    lin = lax.axis_index("section") * n_ten + ten
    n_lin = n_sec * n_ten

    def seq_peer(i):
        return {"seq": i}

    def ten_peer(i):
        return {"tensor": i}

    def lin_peer(i):
        return {"section": i // n_ten, "tensor": i % n_ten}

    def load(i, src, dst):
        return pltpu.make_async_copy(src, dst, loads.at[i])

    load_small = [
        load(0, dt_in, dt_ref), load(1, r_in, r_ref), load(2, b_in, b_ref), load(3, c_in, c_ref),
    ]
    load_values = load(4, v_in, v_ref)
    load_late = [load(5, g_in, g_ref), load(6, cot_in, cot_ref), load(7, gain_in, gain_ref)]
    for copy in load_small + [load_values] + load_late:
        copy.start()
    barrier = pltpu.get_barrier_semaphore()
    for d in range(1, n_seq):
        pl.semaphore_signal(barrier, inc=1, device_id=seq_peer((seq + d) % n_seq), device_id_type=MESH)
    for d in range(1, n_lin):
        pl.semaphore_signal(barrier, inc=1, device_id=lin_peer((lin + d) % n_lin), device_id_type=MESH)

    def send_all(buf, me, count, peer, ssem, rsem):
        for d in range(1, count):
            pltpu.make_async_remote_copy(
                src_ref=buf.at[me], dst_ref=buf.at[me], send_sem=ssem.at[d - 1], recv_sem=rsem.at[d - 1],
                device_id=peer((me + d) % count), device_id_type=MESH,
            ).start()

    def wait_all(buf, me, count, peer, ssem, rsem):
        for d in range(1, count):
            other = (me + count - d) % count
            desc = pltpu.make_async_remote_copy(
                src_ref=buf.at[me], dst_ref=buf.at[other], send_sem=ssem.at[d - 1], recv_sem=rsem.at[d - 1],
                device_id=peer((me + d) % count), device_id_type=MESH,
            )
            desc.wait_send()
            desc.wait_recv()

    def total_of(buf, count):
        out = buf[0]
        for i in range(1, count):
            out = out + buf[i]
        return out

    def at(c):
        return pl.ds(pl.multiple_of(c * width, width), width)

    def loop(body):
        def step(c, carry):
            body(c, at(c))
            return carry

        lax.fori_loop(0, chunks, step, 0)

    def picks(rows, c):
        row = lax.broadcasted_iota(jnp.int32, (rows, width), 0) & (heads - 1)
        col = lax.broadcasted_iota(jnp.int32, (rows, width), 1) // P_SIZE + c * (width // P_SIZE)
        return jnp.where(row == col, 1.0, 0.0)

    for copy in load_small:
        copy.wait()
    eye = lax.broadcasted_iota(jnp.int32, (heads, heads), 0) == lax.broadcasted_iota(jnp.int32, (heads, heads), 1)
    rate = jnp.sum(jnp.where(eye, r_ref[...], 0.0), axis=1, keepdims=True)
    dt = dt_ref[...]
    row_t = lax.broadcasted_iota(jnp.int32, (tokens, tokens), 0)
    col_t = lax.broadcasted_iota(jnp.int32, (tokens, tokens), 1)
    lower = row_t >= col_t
    upper = row_t <= col_t
    cum = unstack3(nn(stacked3(-dt * rate).astype(BF16), jnp.where(upper, 1.0, 0.0).astype(BF16)))
    p3 = stacked3(jnp.exp(cum)).T.astype(BF16)
    q3 = stacked3(jnp.exp(-cum) * dt).T.astype(BF16)
    bt[...] = b_ref[...].astype(F32).T.astype(BF16)
    ct[...] = c_ref[...].astype(F32).T.astype(BF16)

    def forward_hop(k):
        cols = pl.ds(pl.multiple_of(k * HOP, HOP), HOP)
        return pltpu.make_async_remote_copy(
            src_ref=sout.at[:, cols], dst_ref=sin.at[:, cols], send_sem=fs.at[k], recv_sem=fr.at[k],
            device_id=seq_peer((seq + 1) % n_seq), device_id_type=MESH,
        )

    def backward_hop(k):
        cols = pl.ds(pl.multiple_of(k * HOP, HOP), HOP)
        return pltpu.make_async_remote_copy(
            src_ref=gout.at[:, cols], dst_ref=gin.at[:, cols], send_sem=bs.at[k], recv_sem=br.at[k],
            device_id=seq_peer((seq + n_seq - 1) % n_seq), device_id_type=MESH,
        )

    def total_decay(cols):
        return pex[tokens - 1 : tokens, cols]

    def hops_of(c):
        per = width // HOP
        return [(c * per + i, pl.ds(pl.multiple_of((c * per + i) * HOP, HOP), HOP)) for i in range(per)]

    def first(c, cols):
        sel = picks(3 * heads, c).astype(BF16)
        pex[:, cols] = nn(p3, sel)
        qx = nn(q3, sel)
        qex[:, cols] = qx
        hi, lo = split2(qx * v_ref[:, cols].astype(F32))
        xhi[:, cols] = hi
        xlo[:, cols] = lo
        bx[:, cols] = nn(bt[...], hi) + nn(bt[...], lo)

        @pl.when(seq == 0)
        def _():
            for k, part in hops_of(c):
                sout[:, part] = total_decay(part) * bx[:, part]
                forward_hop(k).start()

    load_values.wait()
    pl.semaphore_wait(barrier, n_seq - 1 + n_lin - 1)
    loop(first)

    @pl.when(seq == 0)
    def _():
        sin[...] = jnp.zeros_like(sin)

    @pl.when(seq == n_seq - 1)
    def _():
        gin[...] = jnp.zeros_like(gin)

    cb = nt(c_ref[...], b_ref[...])
    hi, lo = split2(jnp.where(lower, cb, 0.0))
    m_hi[...] = hi
    m_lo[...] = lo
    bc = nt(b_ref[...], c_ref[...])
    hi, lo = split2(jnp.where(upper, bc, 0.0))
    mt_hi[...] = hi
    mt_lo[...] = lo

    def second(c, cols):
        gate = g_ref[:, cols].astype(F32)
        sigm = 1.0 / (1.0 + jnp.exp(-gate))
        swi[:, cols] = gate * sigm
        dsw[:, cols] = sigm * (1.0 + gate * (1.0 - sigm))
        x_hi = xhi[:, cols]
        mix[:, cols] = nn(m_hi[...], x_hi) + (nn(m_hi[...], xlo[:, cols]) + nn(m_lo[...], x_hi))

    for copy in load_late:
        copy.wait()
    loop(second)

    sq[...] = jnp.zeros_like(sq)
    inn[...] = jnp.zeros_like(inn)

    def third(c, cols):
        @pl.when(seq > 0)
        def _():
            for k, part in hops_of(c):
                forward_hop(k).wait_recv()

                @pl.when(seq < n_seq - 1)
                def _():
                    sout[:, part] = total_decay(part) * (sin[:, part] + bx[:, part])
                    forward_hop(k).start()

        hi, lo = split2(sin[:, cols])
        mixed = pex[:, cols] * (mix[:, cols] + (nn(c_ref[...], hi) + nn(c_ref[...], lo)))
        mix[:, cols] = mixed
        gated = mixed * swi[:, cols]
        squares = gated * gated
        products = cot_ref[:, cols].astype(F32) * gain_ref[:, cols] * gated
        for part in range(width // HOP):
            piece = slice(part * HOP, (part + 1) * HOP)
            sq[...] += squares[:, piece]
            inn[...] += products[:, piece]

    loop(third)

    lane = lax.broadcasted_iota(jnp.int32, (tokens, 128), 1)
    stb[ten] = jnp.where(
        lane < 64, jnp.sum(sq[...], axis=1, keepdims=True), jnp.sum(inn[...], axis=1, keepdims=True)
    )
    send_all(stb, ten, n_ten, ten_peer, st_s, st_r)
    wait_all(stb, ten, n_ten, ten_peer, st_s, st_r)
    sums = total_of(stb, n_ten)
    group_width = channels * n_ten
    scale = lax.rsqrt(sums[:, 0:1] / group_width + EPSILON)
    pull = scale * scale * scale * sums[:, 64:65] / group_width

    def fourth(c, cols):
        mixed = mix[:, cols]
        swish = swi[:, cols]
        gated = mixed * swish
        d_gated = scale * (cot_ref[:, cols].astype(F32) * gain_ref[:, cols]) - gated * pull
        gg_ref[:, cols] = (d_gated * mixed * dsw[:, cols]).astype(BF16)
        d_mixed = d_gated * swish
        zd[:, cols] = d_mixed * mixed
        hi, lo = split2(pex[:, cols] * d_mixed)
        ehi[:, cols] = hi
        elo[:, cols] = lo
        ce[:, cols] = nn(ct[...], hi) + nn(ct[...], lo)

        @pl.when(seq == n_seq - 1)
        def _():
            for k, part in hops_of(c):
                gout[:, part] = ce[:, part]
                backward_hop(k).start()

    loop(fourth)

    dm[...] = jnp.zeros_like(dm)
    dca[...] = jnp.zeros_like(dca)

    def fifth(c, cols):
        e_hi = ehi[:, cols]
        e_lo = elo[:, cols]
        x_hi = xhi[:, cols]
        mte[:, cols] = nn(mt_hi[...], e_hi) + (nn(mt_hi[...], e_lo) + nn(mt_lo[...], e_hi))
        dm[...] += nt(e_hi, x_hi) + (nt(e_hi, xlo[:, cols]) + nt(e_lo, x_hi))
        s_hi, s_lo = split2(sin[:, cols])
        dca[...] += nt(e_hi, s_hi) + (nt(e_hi, s_lo) + nt(e_lo, s_hi))
        normed = mix[:, cols] * swi[:, cols] * scale
        res_ref[:, cols] = (normed * gain_ref[:, cols]).astype(BF16)
        gain_sum = jnp.sum(cot_ref[:, cols].astype(F32) * normed, axis=0, keepdims=True)
        gainb[seq, :, cols] = jnp.broadcast_to(gain_sum, (8, width))

    loop(fifth)
    send_all(gainb, seq, n_seq, seq_peer, ga_s, ga_r)
    d_m = jnp.where(lower, dm[...], 0.0)
    hi, lo = split2(d_m)
    dcb[ten] = dca[...] + (nn(hi, b_ref[...]) + nn(lo, b_ref[...]))
    send_all(dcb, ten, n_ten, ten_peer, dc_s, dc_r)
    hi, lo = split2(d_m.T)
    dba[...] = nn(hi, c_ref[...]) + nn(lo, c_ref[...])

    def sixth(c, carry):
        cols = at(c)
        row_sum, direct, end = carry

        @pl.when(seq < n_seq - 1)
        def _():
            for k, part in hops_of(c):
                backward_hop(k).wait_recv()

                @pl.when(seq > 0)
                def _():
                    gout[:, part] = ce[:, part] + total_decay(part) * gin[:, part]
                    backward_hop(k).start()

        e_grad = total_decay(cols) * gin[:, cols]
        hi, lo = split2(e_grad)
        d_v = qex[:, cols] * (mte[:, cols] + (nn(b_ref[...], hi) + nn(b_ref[...], lo)))
        gv_ref[:, cols] = d_v.astype(BF16)
        x_hi = xhi[:, cols]
        dba[...] += nt(x_hi, hi) + (nt(x_hi, lo) + nt(xlo[:, cols], hi))
        own = d_v * v_ref[:, cols].astype(F32)
        sel = picks(heads, c)
        pick = sel.astype(BF16)
        a, b, d = split3(zd[:, cols] - own)
        row_sum = row_sum + (nt(pick, a.astype(BF16)) + nt(pick, b.astype(BF16)) + nt(pick, d.astype(BF16)))
        hi, lo = split2(own)
        direct = direct + (nt(pick, hi) + nt(pick, lo))
        column = jnp.sum(e_grad * (sin[:, cols] + bx[:, cols]), axis=0, keepdims=True)
        end = end + jnp.sum(sel * column, axis=1, keepdims=True)
        return row_sum, direct, end

    zero = jnp.zeros((heads, tokens), F32)
    row_sum, direct, end = lax.fori_loop(0, chunks, sixth, (zero, zero, jnp.zeros((heads, 1), F32)))
    dbb[ten] = dba[...]
    send_all(dbb, ten, n_ten, ten_peer, db_s, db_r)
    tail = unstack3(nn(stacked3(row_sum).astype(BF16), jnp.where(lower, 1.0, 0.0).astype(BF16))) + end
    rateb[seq] = jnp.broadcast_to(-jnp.sum(dt * tail, axis=1, keepdims=True), (heads, 128))
    send_all(rateb, seq, n_seq, seq_peer, ra_s, ra_r)
    gs_ref[...] = direct / dt - rate * tail
    wait_all(gainb, seq, n_seq, seq_peer, ga_s, ga_r)
    gain_total = total_of(gainb, n_seq)[0:1]
    gain_square = jnp.sum(gain_total * gain_total, axis=1, keepdims=True)
    wait_all(rateb, seq, n_seq, seq_peer, ra_s, ra_r)
    rate_total = total_of(rateb, n_seq)
    scb[lin] = jnp.broadcast_to(jnp.sum(rate_total * rate_total, axis=0, keepdims=True) + gain_square, (8, 128))
    send_all(scb, lin, n_lin, lin_peer, sc_s, sc_r)
    wait_all(dcb, ten, n_ten, ten_peer, dc_s, dc_r)
    gc_ref[...] = total_of(dcb, n_ten)
    wait_all(dbb, ten, n_ten, ten_peer, db_s, db_r)
    gb_ref[...] = total_of(dbb, n_ten)

    @pl.when(seq < n_seq - 1)
    def _():
        for k in range(hops):
            forward_hop(k).wait_send()

    @pl.when(seq > 0)
    def _():
        for k in range(hops):
            backward_hop(k).wait_send()

    wait_all(scb, lin, n_lin, lin_peer, sc_s, sc_r)
    total = total_of(scb, n_lin)
    factor = CLIP / jnp.maximum(jnp.sqrt(total), CLIP)
    ggain_ref[...] = gain_total * factor[0:1, 0:1]
    gr_ref[...] = jnp.sum(jnp.where(eye, (rate_total * factor[0:1])[:, 0:heads], 0.0), axis=0, keepdims=True)


def write_out(*refs):
    here, arrived, done = refs[16:24], refs[24], refs[25]
    loads = [pltpu.make_async_copy(refs[i], here[i], arrived.at[i]) for i in range(8)]
    stores = [pltpu.make_async_copy(here[i], refs[8 + i], done.at[i]) for i in range(8)]
    for load in loads:
        load.start()
    for load, store in zip(loads, stores):
        load.wait()
        store.start()
    for store in stores:
        store.wait()


def local(values, gate_in, b_proj, c_proj, step_size, decay_rate, norm_gain, cotangent):
    n_sec, n_seq, n_ten = lax.axis_size("section"), lax.axis_size("seq"), lax.axis_size("tensor")
    n_lin = n_sec * n_ten
    tokens, channels = values.shape
    heads = decay_rate.shape[0]
    hops = channels // HOP
    shape = jax.ShapeDtypeStruct
    vm = pltpu.VMEM
    wide32 = vm((tokens, channels), F32)
    wide16 = vm((tokens, channels), BF16)
    state = vm((N, channels), F32)
    square16 = vm((tokens, tokens), BF16)
    slim = vm((tokens, 128), F32)
    sems = pltpu.SemaphoreType.DMA
    outs = pl.pallas_call(
        functools.partial(kernel, (n_sec, n_seq, n_ten)),
        out_shape=(
            shape((tokens, channels), BF16),
            shape((tokens, channels), BF16),
            shape((tokens, channels), BF16),
            shape((tokens, N), F32),
            shape((tokens, N), F32),
            shape((heads, tokens), F32),
            shape((1, heads), F32),
            shape((1, channels), F32),
        ),
        in_specs=[pl.BlockSpec(memory_space=pltpu.HBM)] * 8,
        out_specs=[pl.BlockSpec(memory_space=vm)] * 8,
        scratch_shapes=[
            wide32, wide32, wide16, wide16, wide16, wide16, wide32, wide32, wide32, wide32, wide32,
            state, state, state, state, state, state, slim, slim, vm((tokens, tokens), F32), slim, slim,
            vm((N, tokens), BF16), vm((N, tokens), BF16), square16, square16, square16, square16,
            vm((n_ten, tokens, 128), F32), vm((n_ten, tokens, 128), F32), vm((n_ten, tokens, 128), F32),
            vm((n_seq, 8, channels), F32), vm((n_seq, heads, 128), F32), vm((n_lin, 8, 128), F32),
            vm((tokens, channels), BF16), vm((tokens, channels), BF16), vm((tokens, N), BF16), vm((tokens, N), BF16),
            vm((heads, tokens), F32), vm((1, heads), F32), vm((1, channels), F32), vm((tokens, channels), BF16),
            sems((8,)),
            sems((hops,)), sems((hops,)), sems((hops,)), sems((hops,)),
            sems((n_ten,)), sems((n_ten,)), sems((n_ten,)), sems((n_ten,)), sems((n_ten,)), sems((n_ten,)),
            sems((n_seq,)), sems((n_seq,)), sems((n_seq,)), sems((n_seq,)), sems((n_lin,)), sems((n_lin,)),
        ],
        compiler_params=pltpu.CompilerParams(
            collective_id=0, has_side_effects=True, vmem_limit_bytes=56 * 1024 * 1024
        ),
    )(
        values, gate_in, b_proj[:, 0, :], c_proj[:, 0, :], step_size,
        decay_rate[None, :], norm_gain[None, :], cotangent,
    )
    result, grad_values, grad_gate, grad_b, grad_c, grad_step, grad_rate, grad_gain = pl.pallas_call(
        write_out,
        out_shape=tuple(shape(x.shape, x.dtype) for x in outs),
        in_specs=[pl.BlockSpec(memory_space=pl.ANY)] * 8,
        out_specs=[pl.BlockSpec(memory_space=pl.ANY)] * 8,
        scratch_shapes=[vm(x.shape, x.dtype) for x in outs] + [sems((8,)), sems((8,))],
        compiler_params=pltpu.CompilerParams(vmem_limit_bytes=56 * 1024 * 1024),
    )(*outs)
    return (
        result, grad_values, grad_gate, grad_b[:, None, :], grad_c[:, None, :], grad_step,
        grad_rate[0], grad_gain[0],
    )


def solution(mesh):
    return jax.shard_map(
        local,
        mesh=mesh,
        in_specs=(
            P("seq", ("section", "tensor")),
            P("seq", ("section", "tensor")),
            P("seq", "section", None),
            P("seq", "section", None),
            P(("section", "tensor"), "seq"),
            P(("section", "tensor")),
            P(("section", "tensor")),
            P("seq", ("section", "tensor")),
        ),
        out_specs=(
            P("seq", ("section", "tensor")),
            P("seq", ("section", "tensor")),
            P("seq", ("section", "tensor")),
            P("seq", "section", None),
            P("seq", "section", None),
            P(("section", "tensor"), "seq"),
            P(("section", "tensor")),
            P(("section", "tensor")),
        ),
        check_vma=False,
    )
```

```python
import functools
import jax
import jax.numpy as jnp
from jax import lax
from jax.experimental import pallas as pl
from jax.experimental.pallas import tpu as pltpu
from jax.sharding import PartitionSpec as P

P_SIZE = 64
N = 128
EPSILON = 1e-05
CLIP = 90.0
WIDE = 256
HOP = 128
ROWS = 32
F32 = jnp.float32
BF16 = jnp.bfloat16
MESH = pl.DeviceIdType.MESH


def nn(a, b):
    return lax.dot_general(a, b, (((1,), (0,)), ((), ())), preferred_element_type=F32)


def nt(a, b):
    return lax.dot_general(a, b, (((1,), (1,)), ((), ())), preferred_element_type=F32)


def split2(x):
    hi = x.astype(BF16)
    return hi, (x - hi.astype(F32)).astype(BF16)


def split3(x):
    hi = x.astype(BF16).astype(F32)
    rest = x - hi
    mid = rest.astype(BF16).astype(F32)
    return hi, mid, rest - mid


def stacked3(x):
    return jnp.concatenate(split3(x), axis=0)


def unstack3(x):
    h = x.shape[0] // 3
    return x[0:h] + x[h : 2 * h] + x[2 * h :]


def kernel(
    sizes,
    v_in, g_in, b_in, c_in, dt_in, r_in, gain_in, cot_in,
    res_ref, gv_ref, gg_ref, gb_ref, gc_ref, gs_ref, gr_ref, ggain_ref,
    pex, qex, xhi, xlo, ehi, elo, mix, zd, mte, swi, dsw,
    bx, sin, sout, ce, gin, gout, sq, inn, dm, dca, dba,
    bt, ct, m_hi, m_lo, mt_hi, mt_lo,
    stb, dcb, dbb, gainb, rateb, scb,
    v_ref, g_ref, b_ref, c_ref, dt_ref, r_ref, gain_ref, cot_ref, loads,
    fs, fr, bs, br, st_s, st_r, dc_s, dc_r, db_s, db_r, ga_s, ga_r, ra_s, ra_r, sc_s, sc_r,
):
    n_sec, n_seq, n_ten = sizes
    tokens, channels = v_ref.shape
    heads = dt_ref.shape[0]
    width = WIDE if channels % WIDE == 0 else HOP
    chunks = channels // width
    hops = channels // HOP * (N // ROWS)
    seq = lax.axis_index("seq")
    ten = lax.axis_index("tensor")
    lin = lax.axis_index("section") * n_ten + ten
    n_lin = n_sec * n_ten

    def seq_peer(i):
        return {"seq": i}

    def ten_peer(i):
        return {"tensor": i}

    def lin_peer(i):
        return {"section": i // n_ten, "tensor": i % n_ten}

    def load(i, src, dst):
        return pltpu.make_async_copy(src, dst, loads.at[i])

    load_small = [
        load(0, dt_in, dt_ref), load(1, r_in, r_ref), load(2, b_in, b_ref), load(3, c_in, c_ref),
    ]
    load_values = load(4, v_in, v_ref)
    load_late = [load(5, g_in, g_ref), load(6, cot_in, cot_ref), load(7, gain_in, gain_ref)]
    for copy in load_small + [load_values] + load_late:
        copy.start()
    barrier = pltpu.get_barrier_semaphore()
    for d in range(1, n_seq):
        pl.semaphore_signal(barrier, inc=1, device_id=seq_peer((seq + d) % n_seq), device_id_type=MESH)
    for d in range(1, n_lin):
        pl.semaphore_signal(barrier, inc=1, device_id=lin_peer((lin + d) % n_lin), device_id_type=MESH)

    def send_all(buf, me, count, peer, ssem, rsem):
        for d in range(1, count):
            pltpu.make_async_remote_copy(
                src_ref=buf.at[me], dst_ref=buf.at[me], send_sem=ssem.at[d - 1], recv_sem=rsem.at[d - 1],
                device_id=peer((me + d) % count), device_id_type=MESH,
            ).start()

    def wait_all(buf, me, count, peer, ssem, rsem):
        for d in range(1, count):
            other = (me + count - d) % count
            desc = pltpu.make_async_remote_copy(
                src_ref=buf.at[me], dst_ref=buf.at[other], send_sem=ssem.at[d - 1], recv_sem=rsem.at[d - 1],
                device_id=peer((me + d) % count), device_id_type=MESH,
            )
            desc.wait_send()
            desc.wait_recv()

    def total_of(buf, count):
        out = buf[0]
        for i in range(1, count):
            out = out + buf[i]
        return out

    def at(c):
        return pl.ds(pl.multiple_of(c * width, width), width)

    def loop(body):
        def step(c, carry):
            body(c, at(c))
            return carry

        lax.fori_loop(0, chunks, step, 0)

    def picks(rows, c):
        row = lax.broadcasted_iota(jnp.int32, (rows, width), 0) & (heads - 1)
        col = lax.broadcasted_iota(jnp.int32, (rows, width), 1) // P_SIZE + c * (width // P_SIZE)
        return jnp.where(row == col, 1.0, 0.0)

    for copy in load_small:
        copy.wait()
    eye = lax.broadcasted_iota(jnp.int32, (heads, heads), 0) == lax.broadcasted_iota(jnp.int32, (heads, heads), 1)
    rate = jnp.sum(jnp.where(eye, r_ref[...], 0.0), axis=1, keepdims=True)
    dt = dt_ref[...]
    row_t = lax.broadcasted_iota(jnp.int32, (tokens, tokens), 0)
    col_t = lax.broadcasted_iota(jnp.int32, (tokens, tokens), 1)
    lower = row_t >= col_t
    upper = row_t <= col_t
    cum = unstack3(nn(stacked3(-dt * rate).astype(BF16), jnp.where(upper, 1.0, 0.0).astype(BF16)))
    p3 = stacked3(jnp.exp(cum)).T.astype(BF16)
    q3 = stacked3(jnp.exp(-cum) * dt).T.astype(BF16)
    bt[...] = b_ref[...].astype(F32).T.astype(BF16)
    ct[...] = c_ref[...].astype(F32).T.astype(BF16)

    def piece_of(k):
        per = N // ROWS
        return pl.ds(pl.multiple_of(k % per * ROWS, ROWS), ROWS), pl.ds(pl.multiple_of(k // per * HOP, HOP), HOP)

    def forward_hop(k):
        return pltpu.make_async_remote_copy(
            src_ref=sout.at[piece_of(k)], dst_ref=sin.at[piece_of(k)], send_sem=fs.at[k], recv_sem=fr.at[k],
            device_id=seq_peer((seq + 1) % n_seq), device_id_type=MESH,
        )

    def backward_hop(k):
        return pltpu.make_async_remote_copy(
            src_ref=gout.at[piece_of(k)], dst_ref=gin.at[piece_of(k)], send_sem=bs.at[k], recv_sem=br.at[k],
            device_id=seq_peer((seq + n_seq - 1) % n_seq), device_id_type=MESH,
        )

    def total_decay(cols):
        return pex[tokens - 1 : tokens, cols]

    def hops_of(c):
        per = width // HOP * (N // ROWS)
        return [(c * per + i, piece_of(c * per + i)) for i in range(per)]

    def first(c, cols):
        sel = picks(3 * heads, c).astype(BF16)
        pex[:, cols] = nn(p3, sel)
        qx = nn(q3, sel)
        qex[:, cols] = qx
        hi, lo = split2(qx * v_ref[:, cols].astype(F32))
        xhi[:, cols] = hi
        xlo[:, cols] = lo
        bx[:, cols] = nn(bt[...], hi) + nn(bt[...], lo)

        @pl.when(seq == 0)
        def _():
            for k, (rows, part) in hops_of(c):
                sout[rows, part] = total_decay(part) * bx[rows, part]
                forward_hop(k).start()

    load_values.wait()
    pl.semaphore_wait(barrier, n_seq - 1 + n_lin - 1)
    loop(first)

    @pl.when(seq == 0)
    def _():
        sin[...] = jnp.zeros_like(sin)

    @pl.when(seq == n_seq - 1)
    def _():
        gin[...] = jnp.zeros_like(gin)

    cb = nt(c_ref[...], b_ref[...])
    hi, lo = split2(jnp.where(lower, cb, 0.0))
    m_hi[...] = hi
    m_lo[...] = lo
    bc = nt(b_ref[...], c_ref[...])
    hi, lo = split2(jnp.where(upper, bc, 0.0))
    mt_hi[...] = hi
    mt_lo[...] = lo

    def second(c, cols):
        gate = g_ref[:, cols].astype(F32)
        sigm = 1.0 / (1.0 + jnp.exp(-gate))
        swi[:, cols] = gate * sigm
        dsw[:, cols] = sigm * (1.0 + gate * (1.0 - sigm))
        x_hi = xhi[:, cols]
        mix[:, cols] = nn(m_hi[...], x_hi) + (nn(m_hi[...], xlo[:, cols]) + nn(m_lo[...], x_hi))

    for copy in load_late:
        copy.wait()
    loop(second)

    sq[...] = jnp.zeros_like(sq)
    inn[...] = jnp.zeros_like(inn)

    def third(c, cols):
        @pl.when(seq > 0)
        def _():
            for k, (rows, part) in hops_of(c):
                forward_hop(k).wait_recv()

                @pl.when(seq < n_seq - 1)
                def _():
                    sout[rows, part] = total_decay(part) * (sin[rows, part] + bx[rows, part])
                    forward_hop(k).start()

        hi, lo = split2(sin[:, cols])
        mixed = pex[:, cols] * (mix[:, cols] + (nn(c_ref[...], hi) + nn(c_ref[...], lo)))
        mix[:, cols] = mixed
        gated = mixed * swi[:, cols]
        squares = gated * gated
        products = cot_ref[:, cols].astype(F32) * gain_ref[:, cols] * gated
        for part in range(width // HOP):
            piece = slice(part * HOP, (part + 1) * HOP)
            sq[...] += squares[:, piece]
            inn[...] += products[:, piece]

    loop(third)

    lane = lax.broadcasted_iota(jnp.int32, (tokens, 128), 1)
    stb[ten] = jnp.where(
        lane < 64, jnp.sum(sq[...], axis=1, keepdims=True), jnp.sum(inn[...], axis=1, keepdims=True)
    )
    send_all(stb, ten, n_ten, ten_peer, st_s, st_r)
    wait_all(stb, ten, n_ten, ten_peer, st_s, st_r)
    sums = total_of(stb, n_ten)
    group_width = channels * n_ten
    scale = lax.rsqrt(sums[:, 0:1] / group_width + EPSILON)
    pull = scale * scale * scale * sums[:, 64:65] / group_width

    def fourth(c, cols):
        mixed = mix[:, cols]
        swish = swi[:, cols]
        gated = mixed * swish
        d_gated = scale * (cot_ref[:, cols].astype(F32) * gain_ref[:, cols]) - gated * pull
        gg_ref[:, cols] = (d_gated * mixed * dsw[:, cols]).astype(BF16)
        d_mixed = d_gated * swish
        zd[:, cols] = d_mixed * mixed
        hi, lo = split2(pex[:, cols] * d_mixed)
        ehi[:, cols] = hi
        elo[:, cols] = lo
        ce[:, cols] = nn(ct[...], hi) + nn(ct[...], lo)

        @pl.when(seq == n_seq - 1)
        def _():
            for k, (rows, part) in hops_of(c):
                gout[rows, part] = ce[rows, part]
                backward_hop(k).start()

    loop(fourth)

    dm[...] = jnp.zeros_like(dm)
    dca[...] = jnp.zeros_like(dca)

    def fifth(c, cols):
        e_hi = ehi[:, cols]
        e_lo = elo[:, cols]
        x_hi = xhi[:, cols]
        mte[:, cols] = nn(mt_hi[...], e_hi) + (nn(mt_hi[...], e_lo) + nn(mt_lo[...], e_hi))
        dm[...] += nt(e_hi, x_hi) + (nt(e_hi, xlo[:, cols]) + nt(e_lo, x_hi))
        s_hi, s_lo = split2(sin[:, cols])
        dca[...] += nt(e_hi, s_hi) + (nt(e_hi, s_lo) + nt(e_lo, s_hi))
        normed = mix[:, cols] * swi[:, cols] * scale
        res_ref[:, cols] = (normed * gain_ref[:, cols]).astype(BF16)
        gain_sum = jnp.sum(cot_ref[:, cols].astype(F32) * normed, axis=0, keepdims=True)
        gainb[seq, :, cols] = jnp.broadcast_to(gain_sum, (8, width))

    loop(fifth)
    send_all(gainb, seq, n_seq, seq_peer, ga_s, ga_r)
    d_m = jnp.where(lower, dm[...], 0.0)
    hi, lo = split2(d_m)
    dcb[ten] = dca[...] + (nn(hi, b_ref[...]) + nn(lo, b_ref[...]))
    send_all(dcb, ten, n_ten, ten_peer, dc_s, dc_r)
    hi, lo = split2(d_m.T)
    dba[...] = nn(hi, c_ref[...]) + nn(lo, c_ref[...])

    def sixth(c, carry):
        cols = at(c)
        row_sum, direct, end = carry

        @pl.when(seq < n_seq - 1)
        def _():
            for k, (rows, part) in hops_of(c):
                backward_hop(k).wait_recv()

                @pl.when(seq > 0)
                def _():
                    gout[rows, part] = ce[rows, part] + total_decay(part) * gin[rows, part]
                    backward_hop(k).start()

        e_grad = total_decay(cols) * gin[:, cols]
        hi, lo = split2(e_grad)
        d_v = qex[:, cols] * (mte[:, cols] + (nn(b_ref[...], hi) + nn(b_ref[...], lo)))
        gv_ref[:, cols] = d_v.astype(BF16)
        x_hi = xhi[:, cols]
        dba[...] += nt(x_hi, hi) + (nt(x_hi, lo) + nt(xlo[:, cols], hi))
        own = d_v * v_ref[:, cols].astype(F32)
        sel = picks(heads, c)
        pick = sel.astype(BF16)
        a, b, d = split3(zd[:, cols] - own)
        row_sum = row_sum + (nt(pick, a.astype(BF16)) + nt(pick, b.astype(BF16)) + nt(pick, d.astype(BF16)))
        hi, lo = split2(own)
        direct = direct + (nt(pick, hi) + nt(pick, lo))
        column = jnp.sum(e_grad * (sin[:, cols] + bx[:, cols]), axis=0, keepdims=True)
        end = end + jnp.sum(sel * column, axis=1, keepdims=True)
        return row_sum, direct, end

    zero = jnp.zeros((heads, tokens), F32)
    row_sum, direct, end = lax.fori_loop(0, chunks, sixth, (zero, zero, jnp.zeros((heads, 1), F32)))
    dbb[ten] = dba[...]
    send_all(dbb, ten, n_ten, ten_peer, db_s, db_r)
    tail = unstack3(nn(stacked3(row_sum).astype(BF16), jnp.where(lower, 1.0, 0.0).astype(BF16))) + end
    rateb[seq] = jnp.broadcast_to(-jnp.sum(dt * tail, axis=1, keepdims=True), (heads, 128))
    send_all(rateb, seq, n_seq, seq_peer, ra_s, ra_r)
    gs_ref[...] = direct / dt - rate * tail
    wait_all(gainb, seq, n_seq, seq_peer, ga_s, ga_r)
    gain_total = total_of(gainb, n_seq)[0:1]
    gain_square = jnp.sum(gain_total * gain_total, axis=1, keepdims=True)
    wait_all(rateb, seq, n_seq, seq_peer, ra_s, ra_r)
    rate_total = total_of(rateb, n_seq)
    scb[lin] = jnp.broadcast_to(jnp.sum(rate_total * rate_total, axis=0, keepdims=True) + gain_square, (8, 128))
    send_all(scb, lin, n_lin, lin_peer, sc_s, sc_r)
    wait_all(dcb, ten, n_ten, ten_peer, dc_s, dc_r)
    gc_ref[...] = total_of(dcb, n_ten)
    wait_all(dbb, ten, n_ten, ten_peer, db_s, db_r)
    gb_ref[...] = total_of(dbb, n_ten)

    @pl.when(seq < n_seq - 1)
    def _():
        lax.fori_loop(0, hops, lambda k, carry: (forward_hop(k).wait_send(), carry)[1], 0)

    @pl.when(seq > 0)
    def _():
        lax.fori_loop(0, hops, lambda k, carry: (backward_hop(k).wait_send(), carry)[1], 0)

    wait_all(scb, lin, n_lin, lin_peer, sc_s, sc_r)
    total = total_of(scb, n_lin)
    factor = CLIP / jnp.maximum(jnp.sqrt(total), CLIP)
    ggain_ref[...] = gain_total * factor[0:1, 0:1]
    gr_ref[...] = jnp.sum(jnp.where(eye, (rate_total * factor[0:1])[:, 0:heads], 0.0), axis=0, keepdims=True)


def write_out(*refs):
    here, arrived, done = refs[16:24], refs[24], refs[25]
    loads = [pltpu.make_async_copy(refs[i], here[i], arrived.at[i]) for i in range(8)]
    stores = [pltpu.make_async_copy(here[i], refs[8 + i], done.at[i]) for i in range(8)]
    for load in loads:
        load.start()
    for load, store in zip(loads, stores):
        load.wait()
        store.start()
    for store in stores:
        store.wait()


def local(values, gate_in, b_proj, c_proj, step_size, decay_rate, norm_gain, cotangent):
    n_sec, n_seq, n_ten = lax.axis_size("section"), lax.axis_size("seq"), lax.axis_size("tensor")
    n_lin = n_sec * n_ten
    tokens, channels = values.shape
    heads = decay_rate.shape[0]
    hops = channels // HOP * (N // ROWS)
    shape = jax.ShapeDtypeStruct
    vm = pltpu.VMEM
    wide32 = vm((tokens, channels), F32)
    wide16 = vm((tokens, channels), BF16)
    state = vm((N, channels), F32)
    square16 = vm((tokens, tokens), BF16)
    slim = vm((tokens, 128), F32)
    sems = pltpu.SemaphoreType.DMA
    outs = pl.pallas_call(
        functools.partial(kernel, (n_sec, n_seq, n_ten)),
        out_shape=(
            shape((tokens, channels), BF16),
            shape((tokens, channels), BF16),
            shape((tokens, channels), BF16),
            shape((tokens, N), F32),
            shape((tokens, N), F32),
            shape((heads, tokens), F32),
            shape((1, heads), F32),
            shape((1, channels), F32),
        ),
        in_specs=[pl.BlockSpec(memory_space=pltpu.HBM)] * 8,
        out_specs=[pl.BlockSpec(memory_space=vm)] * 8,
        scratch_shapes=[
            wide32, wide32, wide16, wide16, wide16, wide16, wide32, wide32, wide32, wide32, wide32,
            state, state, state, state, state, state, slim, slim, vm((tokens, tokens), F32), slim, slim,
            vm((N, tokens), BF16), vm((N, tokens), BF16), square16, square16, square16, square16,
            vm((n_ten, tokens, 128), F32), vm((n_ten, tokens, 128), F32), vm((n_ten, tokens, 128), F32),
            vm((n_seq, 8, channels), F32), vm((n_seq, heads, 128), F32), vm((n_lin, 8, 128), F32),
            vm((tokens, channels), BF16), vm((tokens, channels), BF16), vm((tokens, N), BF16), vm((tokens, N), BF16),
            vm((heads, tokens), F32), vm((1, heads), F32), vm((1, channels), F32), vm((tokens, channels), BF16),
            sems((8,)),
            sems((hops,)), sems((hops,)), sems((hops,)), sems((hops,)),
            sems((n_ten,)), sems((n_ten,)), sems((n_ten,)), sems((n_ten,)), sems((n_ten,)), sems((n_ten,)),
            sems((n_seq,)), sems((n_seq,)), sems((n_seq,)), sems((n_seq,)), sems((n_lin,)), sems((n_lin,)),
        ],
        compiler_params=pltpu.CompilerParams(
            collective_id=0, has_side_effects=True, vmem_limit_bytes=56 * 1024 * 1024
        ),
    )(
        values, gate_in, b_proj[:, 0, :], c_proj[:, 0, :], step_size,
        decay_rate[None, :], norm_gain[None, :], cotangent,
    )
    result, grad_values, grad_gate, grad_b, grad_c, grad_step, grad_rate, grad_gain = pl.pallas_call(
        write_out,
        out_shape=tuple(shape(x.shape, x.dtype) for x in outs),
        in_specs=[pl.BlockSpec(memory_space=pl.ANY)] * 8,
        out_specs=[pl.BlockSpec(memory_space=pl.ANY)] * 8,
        scratch_shapes=[vm(x.shape, x.dtype) for x in outs] + [sems((8,)), sems((8,))],
        compiler_params=pltpu.CompilerParams(vmem_limit_bytes=56 * 1024 * 1024),
    )(*outs)
    return (
        result, grad_values, grad_gate, grad_b[:, None, :], grad_c[:, None, :], grad_step,
        grad_rate[0], grad_gain[0],
    )


def solution(mesh):
    return jax.shard_map(
        local,
        mesh=mesh,
        in_specs=(
            P("seq", ("section", "tensor")),
            P("seq", ("section", "tensor")),
            P("seq", "section", None),
            P("seq", "section", None),
            P(("section", "tensor"), "seq"),
            P(("section", "tensor")),
            P(("section", "tensor")),
            P("seq", ("section", "tensor")),
        ),
        out_specs=(
            P("seq", ("section", "tensor")),
            P("seq", ("section", "tensor")),
            P("seq", ("section", "tensor")),
            P("seq", "section", None),
            P("seq", "section", None),
            P(("section", "tensor"), "seq"),
            P(("section", "tensor")),
            P(("section", "tensor")),
        ),
        check_vma=False,
    )
```

```python
import functools
import jax
import jax.numpy as jnp
from jax import lax
from jax.experimental import pallas as pl
from jax.experimental.pallas import tpu as pltpu
from jax.sharding import PartitionSpec as P

P_SIZE = 64
N = 128
EPSILON = 1e-05
CLIP = 90.0
WIDE = 256
HOP = 128
ROWS = 32
F32 = jnp.float32
BF16 = jnp.bfloat16
MESH = pl.DeviceIdType.MESH


def nn(a, b):
    return lax.dot_general(a, b, (((1,), (0,)), ((), ())), preferred_element_type=F32)


def nt(a, b):
    return lax.dot_general(a, b, (((1,), (1,)), ((), ())), preferred_element_type=F32)


def split2(x):
    hi = x.astype(BF16)
    return hi, (x - hi.astype(F32)).astype(BF16)


def split3(x):
    hi = x.astype(BF16).astype(F32)
    rest = x - hi
    mid = rest.astype(BF16).astype(F32)
    return hi, mid, rest - mid


def stacked3(x):
    return jnp.concatenate(split3(x), axis=0)


def unstack3(x):
    h = x.shape[0] // 3
    return x[0:h] + x[h : 2 * h] + x[2 * h :]


def kernel(
    sizes,
    v_in, g_in, b_in, c_in, dt_in, r_in, gain_in, cot_in,
    res_ref, gv_ref, gg_ref, gb_ref, gc_ref, gs_ref, gr_ref, ggain_ref,
    pex, qex, xhi, xlo, ehi, elo, mix, zd, mte, swi, dsw,
    bx, sin, sout, ce, gin, gout, sq, inn, dm, dca, dba,
    bt, ct, m_hi, m_lo, mt_hi, mt_lo,
    stb, dcb, dbb, gainb, rateb, scb,
    v_ref, g_ref, b_ref, c_ref, dt_ref, r_ref, gain_ref, cot_ref, loads,
    fs, fr, bs, br, st_s, st_r, dc_s, dc_r, db_s, db_r, ga_s, ga_r, ra_s, ra_r, sc_s, sc_r,
):
    n_sec, n_seq, n_ten = sizes
    tokens, channels = v_ref.shape
    heads = dt_ref.shape[0]
    width = WIDE if channels % WIDE == 0 else HOP
    chunks = channels // width
    hops = channels // HOP * (N // ROWS)
    seq = lax.axis_index("seq")
    ten = lax.axis_index("tensor")
    lin = lax.axis_index("section") * n_ten + ten
    n_lin = n_sec * n_ten

    def seq_peer(i):
        return {"seq": i}

    def ten_peer(i):
        return {"tensor": i}

    def lin_peer(i):
        return {"section": i // n_ten, "tensor": i % n_ten}

    def load(i, src, dst):
        return pltpu.make_async_copy(src, dst, loads.at[i])

    load_small = [
        load(0, dt_in, dt_ref), load(1, r_in, r_ref), load(2, b_in, b_ref), load(3, c_in, c_ref),
    ]
    load_values = load(4, v_in, v_ref)
    load_late = [load(5, g_in, g_ref), load(6, cot_in, cot_ref), load(7, gain_in, gain_ref)]
    for copy in load_small + [load_values] + load_late:
        copy.start()
    barrier = pltpu.get_barrier_semaphore()
    for d in range(1, n_seq):
        pl.semaphore_signal(barrier, inc=1, device_id=seq_peer((seq + d) % n_seq), device_id_type=MESH)
    for d in range(1, n_lin):
        pl.semaphore_signal(barrier, inc=1, device_id=lin_peer((lin + d) % n_lin), device_id_type=MESH)

    def send_all(buf, me, count, peer, ssem, rsem):
        for d in range(1, count):
            pltpu.make_async_remote_copy(
                src_ref=buf.at[me], dst_ref=buf.at[me], send_sem=ssem.at[d - 1], recv_sem=rsem.at[d - 1],
                device_id=peer((me + d) % count), device_id_type=MESH,
            ).start()

    def wait_all(buf, me, count, peer, ssem, rsem):
        for d in range(1, count):
            other = (me + count - d) % count
            desc = pltpu.make_async_remote_copy(
                src_ref=buf.at[me], dst_ref=buf.at[other], send_sem=ssem.at[d - 1], recv_sem=rsem.at[d - 1],
                device_id=peer((me + d) % count), device_id_type=MESH,
            )
            desc.wait_send()
            desc.wait_recv()

    def total_of(buf, count):
        out = buf[0]
        for i in range(1, count):
            out = out + buf[i]
        return out

    def at(c):
        return pl.ds(pl.multiple_of(c * width, width), width)

    def loop(body):
        def step(c, carry):
            body(c, at(c))
            return carry

        lax.fori_loop(0, chunks, step, 0)

    def picks(rows, c):
        row = lax.broadcasted_iota(jnp.int32, (rows, width), 0) & (heads - 1)
        col = lax.broadcasted_iota(jnp.int32, (rows, width), 1) // P_SIZE + c * (width // P_SIZE)
        return jnp.where(row == col, 1.0, 0.0)

    for copy in load_small:
        copy.wait()
    eye = lax.broadcasted_iota(jnp.int32, (heads, heads), 0) == lax.broadcasted_iota(jnp.int32, (heads, heads), 1)
    rate = jnp.sum(jnp.where(eye, r_ref[...], 0.0), axis=1, keepdims=True)
    dt = dt_ref[...]
    row_t = lax.broadcasted_iota(jnp.int32, (tokens, tokens), 0)
    col_t = lax.broadcasted_iota(jnp.int32, (tokens, tokens), 1)
    lower = row_t >= col_t
    upper = row_t <= col_t
    cum = unstack3(nn(stacked3(-dt * rate).astype(BF16), jnp.where(upper, 1.0, 0.0).astype(BF16)))
    p3 = stacked3(jnp.exp(cum)).T.astype(BF16)
    q3 = stacked3(jnp.exp(-cum) * dt).T.astype(BF16)
    bt[...] = b_ref[...].astype(F32).T.astype(BF16)
    ct[...] = c_ref[...].astype(F32).T.astype(BF16)

    def piece_of(k):
        per = N // ROWS
        return pl.ds(pl.multiple_of(k % per * ROWS, ROWS), ROWS), pl.ds(pl.multiple_of(k // per * HOP, HOP), HOP)

    def forward_hop(k):
        return pltpu.make_async_remote_copy(
            src_ref=sout.at[piece_of(k)], dst_ref=sin.at[piece_of(k)], send_sem=fs.at[k], recv_sem=fr.at[k],
            device_id=seq_peer((seq + 1) % n_seq), device_id_type=MESH,
        )

    def backward_hop(k):
        return pltpu.make_async_remote_copy(
            src_ref=gout.at[piece_of(k)], dst_ref=gin.at[piece_of(k)], send_sem=bs.at[k], recv_sem=br.at[k],
            device_id=seq_peer((seq + n_seq - 1) % n_seq), device_id_type=MESH,
        )

    def total_decay(cols):
        return pex[tokens - 1 : tokens, cols]

    def hops_of(c):
        per = width // HOP * (N // ROWS)
        return [(c * per + i, piece_of(c * per + i)) for i in range(per)]

    def first(c, cols):
        sel = picks(3 * heads, c).astype(BF16)
        pex[:, cols] = nn(p3, sel)
        qx = nn(q3, sel)
        qex[:, cols] = qx
        hi, lo = split2(qx * v_ref[:, cols].astype(F32))
        xhi[:, cols] = hi
        xlo[:, cols] = lo
        bx[:, cols] = nn(bt[...], hi) + nn(bt[...], lo)

        @pl.when(seq == 0)
        def _():
            for k, (rows, part) in hops_of(c):
                sout[rows, part] = total_decay(part) * bx[rows, part]
                forward_hop(k).start()

    load_values.wait()
    pl.semaphore_wait(barrier, n_seq - 1 + n_lin - 1)
    loop(first)

    @pl.when(seq == 0)
    def _():
        sin[...] = jnp.zeros_like(sin)

    @pl.when(seq == n_seq - 1)
    def _():
        gin[...] = jnp.zeros_like(gin)

    cb = nt(c_ref[...], b_ref[...])
    hi, lo = split2(jnp.where(lower, cb, 0.0))
    m_hi[...] = hi
    m_lo[...] = lo
    bc = nt(b_ref[...], c_ref[...])
    hi, lo = split2(jnp.where(upper, bc, 0.0))
    mt_hi[...] = hi
    mt_lo[...] = lo

    def forward_relay(c):
        for k, (rows, part) in hops_of(c):
            forward_hop(k).wait_recv()

            @pl.when(seq < n_seq - 1)
            def _():
                sout[rows, part] = total_decay(part) * (sin[rows, part] + bx[rows, part])
                forward_hop(k).start()

    def second(c, cols):
        @pl.when((seq > 0) & (2 * seq < n_seq))
        def _():
            forward_relay(c)

        gate = g_ref[:, cols].astype(F32)
        sigm = 1.0 / (1.0 + jnp.exp(-gate))
        swi[:, cols] = gate * sigm
        dsw[:, cols] = sigm * (1.0 + gate * (1.0 - sigm))
        x_hi = xhi[:, cols]
        mix[:, cols] = nn(m_hi[...], x_hi) + (nn(m_hi[...], xlo[:, cols]) + nn(m_lo[...], x_hi))

    for copy in load_late:
        copy.wait()
    loop(second)

    sq[...] = jnp.zeros_like(sq)
    inn[...] = jnp.zeros_like(inn)

    def third(c, cols):
        @pl.when(2 * seq >= n_seq)
        def _():
            forward_relay(c)

        hi, lo = split2(sin[:, cols])
        mixed = pex[:, cols] * (mix[:, cols] + (nn(c_ref[...], hi) + nn(c_ref[...], lo)))
        mix[:, cols] = mixed
        gated = mixed * swi[:, cols]
        squares = gated * gated
        products = cot_ref[:, cols].astype(F32) * gain_ref[:, cols] * gated
        for part in range(width // HOP):
            piece = slice(part * HOP, (part + 1) * HOP)
            sq[...] += squares[:, piece]
            inn[...] += products[:, piece]

    loop(third)

    lane = lax.broadcasted_iota(jnp.int32, (tokens, 128), 1)
    stb[ten] = jnp.where(
        lane < 64, jnp.sum(sq[...], axis=1, keepdims=True), jnp.sum(inn[...], axis=1, keepdims=True)
    )
    send_all(stb, ten, n_ten, ten_peer, st_s, st_r)
    wait_all(stb, ten, n_ten, ten_peer, st_s, st_r)
    sums = total_of(stb, n_ten)
    group_width = channels * n_ten
    scale = lax.rsqrt(sums[:, 0:1] / group_width + EPSILON)
    pull = scale * scale * scale * sums[:, 64:65] / group_width

    def fourth(c, cols):
        mixed = mix[:, cols]
        swish = swi[:, cols]
        gated = mixed * swish
        d_gated = scale * (cot_ref[:, cols].astype(F32) * gain_ref[:, cols]) - gated * pull
        gg_ref[:, cols] = (d_gated * mixed * dsw[:, cols]).astype(BF16)
        d_mixed = d_gated * swish
        zd[:, cols] = d_mixed * mixed
        hi, lo = split2(pex[:, cols] * d_mixed)
        ehi[:, cols] = hi
        elo[:, cols] = lo
        ce[:, cols] = nn(ct[...], hi) + nn(ct[...], lo)

        @pl.when(seq == n_seq - 1)
        def _():
            for k, (rows, part) in hops_of(c):
                gout[rows, part] = ce[rows, part]
                backward_hop(k).start()

    loop(fourth)

    dm[...] = jnp.zeros_like(dm)
    dca[...] = jnp.zeros_like(dca)

    def fifth(c, cols):
        e_hi = ehi[:, cols]
        e_lo = elo[:, cols]
        x_hi = xhi[:, cols]
        mte[:, cols] = nn(mt_hi[...], e_hi) + (nn(mt_hi[...], e_lo) + nn(mt_lo[...], e_hi))
        dm[...] += nt(e_hi, x_hi) + (nt(e_hi, xlo[:, cols]) + nt(e_lo, x_hi))
        s_hi, s_lo = split2(sin[:, cols])
        dca[...] += nt(e_hi, s_hi) + (nt(e_hi, s_lo) + nt(e_lo, s_hi))
        normed = mix[:, cols] * swi[:, cols] * scale
        res_ref[:, cols] = (normed * gain_ref[:, cols]).astype(BF16)
        gain_sum = jnp.sum(cot_ref[:, cols].astype(F32) * normed, axis=0, keepdims=True)
        gainb[seq, :, cols] = jnp.broadcast_to(gain_sum, (8, width))

    loop(fifth)
    send_all(gainb, seq, n_seq, seq_peer, ga_s, ga_r)
    d_m = jnp.where(lower, dm[...], 0.0)
    hi, lo = split2(d_m)
    dcb[ten] = dca[...] + (nn(hi, b_ref[...]) + nn(lo, b_ref[...]))
    send_all(dcb, ten, n_ten, ten_peer, dc_s, dc_r)
    hi, lo = split2(d_m.T)
    dba[...] = nn(hi, c_ref[...]) + nn(lo, c_ref[...])

    def sixth(c, carry):
        cols = at(c)
        row_sum, direct, end = carry

        @pl.when(seq < n_seq - 1)
        def _():
            for k, (rows, part) in hops_of(c):
                backward_hop(k).wait_recv()

                @pl.when(seq > 0)
                def _():
                    gout[rows, part] = ce[rows, part] + total_decay(part) * gin[rows, part]
                    backward_hop(k).start()

        e_grad = total_decay(cols) * gin[:, cols]
        hi, lo = split2(e_grad)
        d_v = qex[:, cols] * (mte[:, cols] + (nn(b_ref[...], hi) + nn(b_ref[...], lo)))
        gv_ref[:, cols] = d_v.astype(BF16)
        x_hi = xhi[:, cols]
        dba[...] += nt(x_hi, hi) + (nt(x_hi, lo) + nt(xlo[:, cols], hi))
        own = d_v * v_ref[:, cols].astype(F32)
        sel = picks(heads, c)
        pick = sel.astype(BF16)
        a, b, d = split3(zd[:, cols] - own)
        row_sum = row_sum + (nt(pick, a.astype(BF16)) + nt(pick, b.astype(BF16)) + nt(pick, d.astype(BF16)))
        hi, lo = split2(own)
        direct = direct + (nt(pick, hi) + nt(pick, lo))
        column = jnp.sum(e_grad * (sin[:, cols] + bx[:, cols]), axis=0, keepdims=True)
        end = end + jnp.sum(sel * column, axis=1, keepdims=True)
        return row_sum, direct, end

    zero = jnp.zeros((heads, tokens), F32)
    row_sum, direct, end = lax.fori_loop(0, chunks, sixth, (zero, zero, jnp.zeros((heads, 1), F32)))
    dbb[ten] = dba[...]
    send_all(dbb, ten, n_ten, ten_peer, db_s, db_r)
    tail = unstack3(nn(stacked3(row_sum).astype(BF16), jnp.where(lower, 1.0, 0.0).astype(BF16))) + end
    rateb[seq] = jnp.broadcast_to(-jnp.sum(dt * tail, axis=1, keepdims=True), (heads, 128))
    send_all(rateb, seq, n_seq, seq_peer, ra_s, ra_r)
    gs_ref[...] = direct / dt - rate * tail
    wait_all(gainb, seq, n_seq, seq_peer, ga_s, ga_r)
    gain_total = total_of(gainb, n_seq)[0:1]
    gain_square = jnp.sum(gain_total * gain_total, axis=1, keepdims=True)
    wait_all(rateb, seq, n_seq, seq_peer, ra_s, ra_r)
    rate_total = total_of(rateb, n_seq)
    scb[lin] = jnp.broadcast_to(jnp.sum(rate_total * rate_total, axis=0, keepdims=True) + gain_square, (8, 128))
    send_all(scb, lin, n_lin, lin_peer, sc_s, sc_r)
    wait_all(dcb, ten, n_ten, ten_peer, dc_s, dc_r)
    gc_ref[...] = total_of(dcb, n_ten)
    wait_all(dbb, ten, n_ten, ten_peer, db_s, db_r)
    gb_ref[...] = total_of(dbb, n_ten)

    @pl.when(seq < n_seq - 1)
    def _():
        lax.fori_loop(0, hops, lambda k, carry: (forward_hop(k).wait_send(), carry)[1], 0)

    @pl.when(seq > 0)
    def _():
        lax.fori_loop(0, hops, lambda k, carry: (backward_hop(k).wait_send(), carry)[1], 0)

    wait_all(scb, lin, n_lin, lin_peer, sc_s, sc_r)
    total = total_of(scb, n_lin)
    factor = CLIP / jnp.maximum(jnp.sqrt(total), CLIP)
    ggain_ref[...] = gain_total * factor[0:1, 0:1]
    gr_ref[...] = jnp.sum(jnp.where(eye, (rate_total * factor[0:1])[:, 0:heads], 0.0), axis=0, keepdims=True)


def write_out(*refs):
    here, arrived, done = refs[16:24], refs[24], refs[25]
    loads = [pltpu.make_async_copy(refs[i], here[i], arrived.at[i]) for i in range(8)]
    stores = [pltpu.make_async_copy(here[i], refs[8 + i], done.at[i]) for i in range(8)]
    for load in loads:
        load.start()
    for load, store in zip(loads, stores):
        load.wait()
        store.start()
    for store in stores:
        store.wait()


def local(values, gate_in, b_proj, c_proj, step_size, decay_rate, norm_gain, cotangent):
    n_sec, n_seq, n_ten = lax.axis_size("section"), lax.axis_size("seq"), lax.axis_size("tensor")
    n_lin = n_sec * n_ten
    tokens, channels = values.shape
    heads = decay_rate.shape[0]
    hops = channels // HOP * (N // ROWS)
    shape = jax.ShapeDtypeStruct
    vm = pltpu.VMEM
    wide32 = vm((tokens, channels), F32)
    wide16 = vm((tokens, channels), BF16)
    state = vm((N, channels), F32)
    square16 = vm((tokens, tokens), BF16)
    slim = vm((tokens, 128), F32)
    sems = pltpu.SemaphoreType.DMA
    outs = pl.pallas_call(
        functools.partial(kernel, (n_sec, n_seq, n_ten)),
        out_shape=(
            shape((tokens, channels), BF16),
            shape((tokens, channels), BF16),
            shape((tokens, channels), BF16),
            shape((tokens, N), F32),
            shape((tokens, N), F32),
            shape((heads, tokens), F32),
            shape((1, heads), F32),
            shape((1, channels), F32),
        ),
        in_specs=[pl.BlockSpec(memory_space=pltpu.HBM)] * 8,
        out_specs=[pl.BlockSpec(memory_space=vm)] * 8,
        scratch_shapes=[
            wide32, wide32, wide16, wide16, wide16, wide16, wide32, wide32, wide32, wide32, wide32,
            state, state, state, state, state, state, slim, slim, vm((tokens, tokens), F32), slim, slim,
            vm((N, tokens), BF16), vm((N, tokens), BF16), square16, square16, square16, square16,
            vm((n_ten, tokens, 128), F32), vm((n_ten, tokens, 128), F32), vm((n_ten, tokens, 128), F32),
            vm((n_seq, 8, channels), F32), vm((n_seq, heads, 128), F32), vm((n_lin, 8, 128), F32),
            vm((tokens, channels), BF16), vm((tokens, channels), BF16), vm((tokens, N), BF16), vm((tokens, N), BF16),
            vm((heads, tokens), F32), vm((1, heads), F32), vm((1, channels), F32), vm((tokens, channels), BF16),
            sems((8,)),
            sems((hops,)), sems((hops,)), sems((hops,)), sems((hops,)),
            sems((n_ten,)), sems((n_ten,)), sems((n_ten,)), sems((n_ten,)), sems((n_ten,)), sems((n_ten,)),
            sems((n_seq,)), sems((n_seq,)), sems((n_seq,)), sems((n_seq,)), sems((n_lin,)), sems((n_lin,)),
        ],
        compiler_params=pltpu.CompilerParams(
            collective_id=0, has_side_effects=True, vmem_limit_bytes=56 * 1024 * 1024
        ),
    )(
        values, gate_in, b_proj[:, 0, :], c_proj[:, 0, :], step_size,
        decay_rate[None, :], norm_gain[None, :], cotangent,
    )
    result, grad_values, grad_gate, grad_b, grad_c, grad_step, grad_rate, grad_gain = pl.pallas_call(
        write_out,
        out_shape=tuple(shape(x.shape, x.dtype) for x in outs),
        in_specs=[pl.BlockSpec(memory_space=pl.ANY)] * 8,
        out_specs=[pl.BlockSpec(memory_space=pl.ANY)] * 8,
        scratch_shapes=[vm(x.shape, x.dtype) for x in outs] + [sems((8,)), sems((8,))],
        compiler_params=pltpu.CompilerParams(vmem_limit_bytes=56 * 1024 * 1024),
    )(*outs)
    return (
        result, grad_values, grad_gate, grad_b[:, None, :], grad_c[:, None, :], grad_step,
        grad_rate[0], grad_gain[0],
    )


def solution(mesh):
    return jax.shard_map(
        local,
        mesh=mesh,
        in_specs=(
            P("seq", ("section", "tensor")),
            P("seq", ("section", "tensor")),
            P("seq", "section", None),
            P("seq", "section", None),
            P(("section", "tensor"), "seq"),
            P(("section", "tensor")),
            P(("section", "tensor")),
            P("seq", ("section", "tensor")),
        ),
        out_specs=(
            P("seq", ("section", "tensor")),
            P("seq", ("section", "tensor")),
            P("seq", ("section", "tensor")),
            P("seq", "section", None),
            P("seq", "section", None),
            P(("section", "tensor"), "seq"),
            P(("section", "tensor")),
            P(("section", "tensor")),
        ),
        check_vma=False,
    )
```
